32 devices in a mesh: row: 4 (over x, core), col: 2 (over y), rep: 4 (over z).
Axes of the slice: x: 2, y: 2, z: 4, core: 2. Of those that a mesh axis runs over, the one named last changes fastest.
Arguments:
- vectors: float32 [8, 1024], P('rep', ('row', 'col')), may hold values from -6 to 6
- energies: float32 [1024], P(('row', 'col')), may hold values from 0 to 16
- tiles: bfloat16 [32, 128, 128], P(('row', 'col', 'rep')), may hold values from -0.375 to 0.375
- tile_codes: int32 [32], P(('row', 'col', 'rep')), may hold values from -1 to 7, as said below
Outputs:
- filtered: float32 [8, 1024], P('rep', ('row', 'col'))
- ritz_values: float32 [8], P('rep')
The draws below stay inside these ranges and needn't reach their ends.
Inputs may be any that keep to these rules, and one draw needn't show every extreme that they name: `tile_codes`: slots of device (row, col, rep) hold tiles of grid cell (row, col) only. A code q stands for block row row * 2 + q // 4 and block column (q % 4) * 2 + col, which lies on or above the diagonal. Each cell holds its diagonal tile, each position at most once; a cell's tiles, in increasing code order, are dealt to its 4 devices in turn, so the occupied slots of a device come first and the rest are -1. Some device fills all 1 slots.
All inputs are finite; a program needn't handle non-finite values.
Results may differ from the reference program's by a relative error of at most 0.002.
Values may be sent and summed in bfloat16 or wider, within the bound.
A program may use at most 64 MiB of HBM per device.

```python
import jax
import jax.numpy as jnp
from jax import lax

TILE = 128
NV = 8
OUTER = 1
PASSES = 1
DEG = 2
NR = 4
NC = 2
NP = 4
NB = 8
NS = 1024
SLOTS = 1


def tile_layout(key):
    cell_total = NR * NC
    cells = jnp.arange(cell_total, dtype=jnp.int32)
    cell_row = cells // NC
    cell_col = cells % NC
    spots = jnp.arange(NB, dtype=jnp.int32)
    block_i = cell_row[:, None] * NC + (spots // NR)[None, :]
    block_j = (spots % NR)[None, :] * NC + cell_col[:, None]
    upper = block_j >= block_i
    diagonal = block_j == block_i
    corner = (cells == NC - 1)[:, None] & (spots == NB - 1)[None, :]
    forced = diagonal | corner
    upper_count = jnp.sum(upper, axis=1).astype(jnp.int32)
    forced_count = jnp.sum(forced, axis=1).astype(jnp.int32)
    density = jax.random.randint(jax.random.fold_in(key, 101), (cell_total,), 80, 301)
    density = jnp.where(cells == NC - 1, 300, density)
    floor_count = jax.random.randint(jax.random.fold_in(key, 303), (cell_total,), 1, 3)
    counts = jnp.maximum(floor_count, density * upper_count // 1000)
    counts = jnp.minimum(counts, jnp.minimum(upper_count, NP * SLOTS))
    counts = jnp.maximum(counts, forced_count)
    subkeys = jax.random.split(jax.random.fold_in(key, 202), cell_total)
    ranks = jax.vmap(lambda subkey: jax.random.permutation(subkey, NB))(subkeys).astype(jnp.int32)
    scores = jnp.where(diagonal, 5 * NB + spots[None, :], jnp.where(forced, 3 * NB + spots[None, :], jnp.where(upper, NB + ranks, -1 - spots[None, :])))
    order = jnp.argsort(-scores, axis=1, stable=True)
    places = jnp.argsort(order, axis=1, stable=True)
    chosen = places < counts[:, None]
    ordered = jnp.sort(jnp.where(chosen, spots[None, :], NB + spots[None, :]), axis=1)
    turns = jnp.arange(SLOTS, dtype=jnp.int32)[None, :] * NP + jnp.arange(NP, dtype=jnp.int32)[:, None]
    picked = ordered[:, jnp.minimum(turns, NB - 1)]
    codes = jnp.where(turns[None, :, :] < counts[:, None, None], picked, -1)
    return codes.reshape(-1).astype(jnp.int32)


def draw_tile_codes(key, part):
    return tile_layout(key)


def levels(key, shape, cuts, low, high):
    gain = 1.0
    for axis_at, parts in cuts:
        draws = jax.random.uniform(jax.random.fold_in(jax.random.fold_in(key, 6), axis_at), (parts,), jnp.float32, low / len(cuts), high / len(cuts))
        gain = gain * jnp.repeat(jnp.exp(draws), shape[axis_at] // parts).reshape((-1,) + (1,) * (len(shape) - 1 - axis_at))
    return gain


def bell_draw(stream_key, extent, width, bound, shards=(), held_as=jnp.bfloat16):
    drawn = jax.random.normal(stream_key, extent, jnp.float32) * width
    if len(shards) > 0:
        drawn = levels(stream_key, extent, shards, -0.22, 0.18) * drawn
    return jnp.clip(drawn, min=-bound, max=bound).astype(held_as)


def setup_inputs(seed: int = 0) -> dict:
    key_of = jax.random.split(jax.random.key(seed), 5)
    vectors = bell_draw(key_of[0], (NV, NS), 1.0, 6.0, ((0, 4), (1, 8)), jnp.float32)
    energies = jnp.clip(16.0 * jax.random.uniform(key_of[1], (NS,), jnp.float32) ** levels(key_of[1], (NS,), ((0, 8),), -0.2, 0.2), 0.0, 16.0)
    tiles = bell_draw(key_of[2], (NR * NC * NP * SLOTS, TILE, TILE), (TILE * NB // 4) ** -0.5, 0.375, ((0, 32),))
    tile_codes = draw_tile_codes(jax.random.fold_in(key_of[4], 71), 0)
    return {"vectors": vectors, "energies": energies, "tiles": tiles, "tile_codes": tile_codes}


filter_low = 5.0
filter_top = 20.0
spectrum_low = -3.0


def reference(vectors, energies, tiles, tile_codes):
    slot_count = tiles.shape[0]
    tile_side = tiles.shape[1]
    cell_index = jnp.arange(slot_count, dtype=jnp.int32) // (NP * SLOTS)
    cell_row = cell_index // NC
    cell_col = cell_index % NC
    present = tile_codes >= 0
    safe_code = jnp.where(present, tile_codes, 0).astype(jnp.int32)
    block_i = (cell_row * NC + safe_code // NR).astype(jnp.int32)
    block_j = ((safe_code % NR) * NC + cell_col).astype(jnp.int32)
    upper_mask = lax.broadcasted_iota(jnp.int32, (tile_side, tile_side), 1) > lax.broadcasted_iota(jnp.int32, (tile_side, tile_side), 0)
    keep_mask = present[:, None, None] & (upper_mask[None] | (block_i != block_j)[:, None, None])
    stored = jnp.where(keep_mask, tiles, jnp.zeros((), tiles.dtype)).astype(jnp.float32)

    def product(vector_block):
        rounded = lax.optimization_barrier(vector_block.astype(jnp.bfloat16)).astype(jnp.float32)
        rounded = rounded.reshape(NV, NB, TILE)
        direct = jnp.einsum("vsj,sij->svi", rounded[:, block_j], stored, precision=lax.Precision.HIGHEST)
        mirror = jnp.einsum("vsi,sij->svj", rounded[:, block_i], stored, precision=lax.Precision.HIGHEST)
        total = jnp.zeros((NB, NV, TILE), jnp.float32).at[block_i].add(direct).at[block_j].add(mirror)
        return energies[None, :] * vector_block + jnp.transpose(total, (1, 0, 2)).reshape(NV, NS)

    half = (filter_top - filter_low) / 2.0
    centre = (filter_top + filter_low) / 2.0
    sigma_first = half / (spectrum_low - centre)
    tau_value = 2.0 / sigma_first
    current = vectors
    ritz = jnp.zeros((NV,), jnp.float32)
    for outer_step in range(OUTER):
        for pass_step in range(PASSES):
            previous = current
            latest = (product(current) - centre * current) * (sigma_first / half)
            sigma_now = sigma_first
            for degree_step in range(1, DEG):
                sigma_next = 1.0 / (tau_value - sigma_now)
                newest = (product(latest) - centre * latest) * (2.0 * sigma_next / half) - (sigma_now * sigma_next) * previous
                previous = latest
                latest = newest
                sigma_now = sigma_next
            current = latest
        image = product(current)
        squares = jnp.sum(current * current, axis=1)
        crossed = jnp.sum(current * image, axis=1)
        ritz = crossed / (squares + 1e-6)
        resid = image - ritz[:, None] * current
        spacing = energies[None, :] - ritz[:, None]
        current = current - spacing / jnp.maximum(spacing * spacing, 1.0) * resid
    return current, ritz
```

```python
import functools

import jax
import jax.numpy as jnp
from jax import lax
from jax.experimental import pallas as pl
from jax.experimental.pallas import tpu as pltpu
from jax.sharding import PartitionSpec as P

filter_low = 5.0
filter_top = 20.0
spectrum_low = -3.0

half = (filter_top - filter_low) / 2.0
centre = (filter_top + filter_low) / 2.0
sigma_first = half / (spectrum_low - centre)
tau_value = 2.0 / sigma_first
sigma_next = 1.0 / (tau_value - sigma_first)

MESH = pl.DeviceIdType.MESH
CODE_ROWS = 16


def fused_kernel(
    rows,
    cols,
    reps,
    vectors_hbm,
    energies_hbm,
    tiles_hbm,
    codes_hbm,
    filtered_ref,
    ritz_ref,
    energies_ref,
    raw_ref,
    codes_ref,
    pack_ref,
    start_ref,
    dense_ref,
    state_ref,
    part_ref,
    local_sems,
    pack_send,
    pack_recv,
    start_send,
    start_recv,
    part_send,
    part_recv,
):
    row = lax.axis_index("row")
    col = lax.axis_index("col")
    rep = lax.axis_index("rep")
    plane = rows * cols
    place = row * cols + col
    slots, side, _ = raw_ref.shape

    def plane_peer(step):
        other = lax.rem(place + step, plane)
        return other, {"row": other // cols, "col": lax.rem(other, cols)}

    def rep_peer(step):
        other = lax.rem(rep + step, reps)
        return other, {"rep": other}

    barrier = pltpu.get_barrier_semaphore()
    for step in range(1, reps):
        pl.semaphore_signal(barrier, inc=1, device_id=rep_peer(step)[1], device_id_type=MESH)
    for step in range(1, plane):
        pl.semaphore_signal(barrier, inc=1, device_id=plane_peer(step)[1], device_id_type=MESH)

    loads = [
        pltpu.make_async_copy(codes_hbm, codes_ref, local_sems.at[0]),
        pltpu.make_async_copy(tiles_hbm, raw_ref, local_sems.at[1]),
        pltpu.make_async_copy(vectors_hbm, start_ref.at[place], local_sems.at[2]),
        pltpu.make_async_copy(energies_hbm, energies_ref, local_sems.at[3]),
    ]
    for load in loads:
        load.start()
    loads[0].wait()
    loads[1].wait()
    line = lax.broadcasted_iota(jnp.int32, (side, side), 0)
    lane = lax.broadcasted_iota(jnp.int32, (side, side), 1)
    diagonal_code = col * rows + row
    for slot in range(slots):
        code = jnp.full((side, side), codes_ref[slot], jnp.int32)
        keep = (code >= 0) & ((lane > line) | (code != diagonal_code))
        tile = jnp.where(keep, raw_ref[slot].astype(jnp.float32), 0.0)
        pack_ref[rep, slot, :side] = tile.astype(jnp.bfloat16)
        pack_ref[rep, slot, side:] = code[:CODE_ROWS].astype(jnp.float32).astype(jnp.bfloat16)
    loads[2].wait()
    loads[3].wait()
    pl.semaphore_wait(barrier, reps - 1 + plane - 1)

    sends = []
    for step in range(1, reps):
        other, device = rep_peer(step)
        copy = pltpu.make_async_remote_copy(
            src_ref=pack_ref.at[rep],
            dst_ref=pack_ref.at[rep],
            send_sem=pack_send.at[step],
            recv_sem=pack_recv.at[rep],
            device_id=device,
            device_id_type=MESH,
        )
        copy.start()
        sends.append(copy)

    def spread(buffer, send_sems, recv_sems):
        for step in range(1, plane):
            other, device = plane_peer(step)
            copy = pltpu.make_async_remote_copy(
                src_ref=buffer.at[place],
                dst_ref=buffer.at[place],
                send_sem=send_sems.at[step],
                recv_sem=recv_sems.at[place],
                device_id=device,
                device_id_type=MESH,
            )
            copy.start()
            sends.append(copy)

    def collect(buffer, recv_sems):
        for step in range(1, plane):
            other, device = plane_peer(step)
            pltpu.make_async_remote_copy(
                src_ref=buffer.at[other],
                dst_ref=buffer.at[other],
                send_sem=recv_sems.at[other],
                recv_sem=recv_sems.at[other],
                device_id=device,
                device_id_type=MESH,
            ).wait_recv()

    spread(start_ref, start_send, start_recv)

    def place_tiles(source, first):
        for slot in range(slots):
            tile = pack_ref[source, slot, :side].reshape(side // CODE_ROWS, CODE_ROWS, side)
            code = pack_ref[source, slot, side:].astype(jnp.float32)
            for a in range(cols):
                for k in range(rows):
                    spot = jnp.where(code == float(a * rows + k), 1.0, 0.0).astype(jnp.bfloat16)
                    term = (tile * spot[None]).reshape(side, side)
                    here = (pl.ds(a * side, side), pl.ds(k * side, side))
                    if first and slot == 0:
                        dense_ref[here] = term
                    else:
                        dense_ref[here] = dense_ref[here] + term

    place_tiles(rep, True)
    collect(start_ref, start_recv)
    for step in range(1, reps):
        other, device = rep_peer(step)
        pltpu.make_async_remote_copy(
            src_ref=pack_ref.at[other],
            dst_ref=pack_ref.at[other],
            send_sem=pack_recv.at[other],
            recv_sem=pack_recv.at[other],
            device_id=device,
            device_id_type=MESH,
        ).wait_recv()
        place_tiles(other, False)

    energies = energies_ref[...]

    def product(phase, state, scale, own_term):
        column_part = jnp.concatenate([state[k * cols + col] for k in range(rows)], axis=1)
        row_part = jnp.concatenate([state[row * cols + a] for a in range(cols)], axis=1)
        direct = lax.dot_general(
            column_part.astype(jnp.bfloat16),
            dense_ref[...],
            (((1,), (1,)), ((), ())),
            preferred_element_type=jnp.float32,
        )
        mirror = lax.dot_general(
            row_part.astype(jnp.bfloat16),
            dense_ref[...],
            (((1,), (0,)), ((), ())),
            preferred_element_type=jnp.float32,
        )
        buffer = part_ref.at[phase]
        for a in range(cols):
            owned = jnp.where(col == a, own_term, 0.0)
            buffer[place, a] = direct[:, a * side : (a + 1) * side] * scale + owned
        for k in range(rows):
            buffer[place, cols + k] = mirror[:, k * side : (k + 1) * side] * scale
        spread(buffer, part_send.at[phase], part_recv.at[phase])
        collect(buffer, part_recv.at[phase])
        totals = []
        for block in range(plane):
            terms = []
            for c in range(cols):
                terms.append(buffer[(block // cols) * cols + c, block % cols])
            for r in range(rows):
                terms.append(buffer[r * cols + block % cols, cols + block // cols])
            total = terms[0]
            for term in terms[1:]:
                total = total + term
            totals.append(total)
        return totals

    scale = sigma_first / half
    start_own = start_ref[place]
    latest = product(0, start_ref, scale, (energies * start_own - centre * start_own) * scale)
    for block in range(plane):
        state_ref[0, block] = latest[block]
    scale = 2.0 * sigma_next / half
    own = state_ref[0, place]
    newest = product(
        1,
        state_ref.at[0],
        scale,
        (energies * own - centre * own) * scale - sigma_first * sigma_next * start_own,
    )
    for block in range(plane):
        state_ref[1, block] = newest[block]
    own = state_ref[1, place]
    image = product(2, state_ref.at[1], 1.0, energies * own)
    for block in range(plane):
        state_ref[2, block] = image[block]
    squares = newest[0] * newest[0]
    crossed = newest[0] * image[0]
    for block in range(1, plane):
        squares = squares + newest[block] * newest[block]
        crossed = crossed + newest[block] * image[block]
    ritz = jnp.sum(crossed, axis=1, keepdims=True) / (
        jnp.sum(squares, axis=1, keepdims=True) + 1e-06
    )
    resid = state_ref[2, place] - ritz * own
    spacing = energies - ritz
    filtered_ref[...] = own - spacing / jnp.maximum(spacing * spacing, 1.0) * resid
    for vector in range(own.shape[0]):
        ritz_ref[vector] = ritz[vector, 0]
    for copy in sends:
        copy.wait_send()


def fused(vectors, energies, tiles, tile_codes):
    rows = lax.axis_size("row")
    cols = lax.axis_size("col")
    reps = lax.axis_size("rep")
    plane = rows * cols
    local_count = vectors.shape[0]
    slots, side, _ = tiles.shape
    vector_shape = (local_count, side)
    return pl.pallas_call(
        functools.partial(fused_kernel, rows, cols, reps),
        out_shape=(
            jax.ShapeDtypeStruct(vector_shape, jnp.float32),
            jax.ShapeDtypeStruct((local_count,), jnp.float32),
        ),
        in_specs=[pl.BlockSpec(memory_space=pl.ANY)] * 4,
        out_specs=(
            pl.BlockSpec(memory_space=pltpu.VMEM),
            pl.BlockSpec(memory_space=pltpu.SMEM),
        ),
        scratch_shapes=[
            pltpu.VMEM((1, side), jnp.float32),
            pltpu.VMEM((slots, side, side), jnp.bfloat16),
            pltpu.SMEM((slots,), jnp.int32),
            pltpu.VMEM((reps, slots, side + CODE_ROWS, side), jnp.bfloat16),
            pltpu.VMEM((plane,) + vector_shape, jnp.float32),
            pltpu.VMEM((cols * side, rows * side), jnp.bfloat16),
            pltpu.VMEM((3, plane) + vector_shape, jnp.float32),
            pltpu.VMEM((3, plane, cols + rows) + vector_shape, jnp.float32),
            pltpu.SemaphoreType.DMA((4,)),
            pltpu.SemaphoreType.DMA((reps,)),
            pltpu.SemaphoreType.DMA((reps,)),
            pltpu.SemaphoreType.DMA((plane,)),
            pltpu.SemaphoreType.DMA((plane,)),
            pltpu.SemaphoreType.DMA((3, plane)),
            pltpu.SemaphoreType.DMA((3, plane)),
        ],
        compiler_params=pltpu.CompilerParams(collective_id=0, has_side_effects=True),
    )(vectors, energies.reshape(1, side), tiles, tile_codes)


def collective_form(vectors, energies, tiles, tile_codes):
    rows_count = lax.axis_size("row")
    cols_count = lax.axis_size("col")
    reps_count = lax.axis_size("rep")
    row_index = lax.axis_index("row")
    col_index = lax.axis_index("col")
    tile_side = tiles.shape[1]
    local_count = vectors.shape[0]
    total_count = local_count * reps_count
    present = tile_codes >= 0
    safe_code = jnp.where(present, tile_codes, 0)
    block_row = safe_code // rows_count
    block_col = safe_code % rows_count
    on_diagonal = present & (block_row == col_index) & (block_col == row_index)
    upper_mask = lax.broadcasted_iota(jnp.int32, (tile_side, tile_side), 1) > lax.broadcasted_iota(
        jnp.int32, (tile_side, tile_side), 0
    )
    keep_mask = present[:, None, None] & (
        upper_mask[None] | jnp.logical_not(on_diagonal)[:, None, None]
    )
    stored = jnp.where(keep_mask, tiles, jnp.zeros((), tiles.dtype))
    row_select = jnp.where(
        present[:, None] & (block_row[:, None] == jnp.arange(cols_count)[None, :]), 1.0, 0.0
    ).astype(jnp.float32)
    col_select = jnp.where(
        present[:, None] & (block_col[:, None] == jnp.arange(rows_count)[None, :]), 1.0, 0.0
    ).astype(jnp.float32)

    def chosen(select, group):
        picked = jnp.einsum(
            "sk,kvj->svj",
            select.astype(group.dtype),
            group,
            preferred_element_type=jnp.float32,
        )
        return picked.astype(group.dtype)

    def product(vector_block):
        rounded = vector_block.astype(jnp.bfloat16)[None]
        row_group = lax.all_gather(rounded, ("col", "rep"), axis=0, tiled=True).reshape(
            cols_count, total_count, tile_side
        )
        col_group = lax.all_gather(rounded, ("row", "rep"), axis=0, tiled=True).reshape(
            rows_count, total_count, tile_side
        )
        direct = jnp.einsum(
            "svj,sij->svi", chosen(col_select, col_group), stored, preferred_element_type=jnp.float32
        )
        mirror = jnp.einsum(
            "svi,sij->svj", chosen(row_select, row_group), stored, preferred_element_type=jnp.float32
        )
        row_terms = jnp.einsum("sa,svi->avi", row_select, direct, precision=lax.Precision.HIGHEST)
        col_terms = jnp.einsum("sk,svj->kvj", col_select, mirror, precision=lax.Precision.HIGHEST)
        row_total = lax.psum_scatter(
            row_terms.reshape(cols_count * reps_count, local_count, tile_side),
            ("col", "rep"),
            scatter_dimension=0,
            tiled=True,
        )[0]
        partial_rows = lax.psum_scatter(col_terms, "row", scatter_dimension=0, tiled=True)
        col_total = lax.psum_scatter(partial_rows, "rep", scatter_dimension=1, tiled=True)[0]
        return energies[None, :] * vector_block + row_total + col_total

    half = (filter_top - filter_low) / 2.0
    centre = (filter_top + filter_low) / 2.0
    sigma_first = half / (spectrum_low - centre)
    tau_value = 2.0 / sigma_first
    current = vectors
    previous = current
    latest = (product(current) - centre * current) * (sigma_first / half)
    sigma_next = 1.0 / (tau_value - sigma_first)
    newest = (product(latest) - centre * latest) * (
        2.0 * sigma_next / half
    ) - sigma_first * sigma_next * previous
    current = newest
    image = product(current)
    squares, crossed = lax.psum(
        (jnp.sum(current * current, axis=1), jnp.sum(current * image, axis=1)), ("row", "col")
    )
    ritz = crossed / (squares + 1e-06)
    resid = image - ritz[:, None] * current
    spacing = energies[None, :] - ritz[:, None]
    current = current - spacing / jnp.maximum(spacing * spacing, 1.0) * resid
    return (current, ritz)


def on_device(vectors, energies, tiles, tile_codes):
    plane = lax.axis_size("row") * lax.axis_size("col")
    placed = lax.axis_size("rep") * tiles.shape[0] * plane
    if placed <= 256 and energies.shape[0] == tiles.shape[1]:
        return fused(vectors, energies, tiles, tile_codes)
    return collective_form(vectors, energies, tiles, tile_codes)


def solution(mesh):
    in_specs = (
        P("rep", ("row", "col")),
        P(("row", "col")),
        P(("row", "col", "rep"), None, None),
        P(("row", "col", "rep")),
    )
    out_specs = (P("rep", ("row", "col")), P("rep"))
    return jax.shard_map(
        on_device, mesh=mesh, in_specs=in_specs, out_specs=out_specs, check_vma=False
    )
```

```python
import functools

import jax
import jax.numpy as jnp
from jax import lax
from jax.experimental import pallas as pl
from jax.experimental.pallas import tpu as pltpu
from jax.sharding import PartitionSpec as P

filter_low = 5.0
filter_top = 20.0
spectrum_low = -3.0

half = (filter_top - filter_low) / 2.0
centre = (filter_top + filter_low) / 2.0
sigma_first = half / (spectrum_low - centre)
tau_value = 2.0 / sigma_first
sigma_next = 1.0 / (tau_value - sigma_first)

MESH = pl.DeviceIdType.MESH
CODE_ROWS = 16


def fused_kernel(
    rows,
    cols,
    reps,
    vectors_hbm,
    energies_hbm,
    tiles_hbm,
    codes_hbm,
    result_ref,
    energies_ref,
    raw_ref,
    codes_ref,
    pack_ref,
    start_ref,
    dense_ref,
    state_ref,
    part_ref,
    local_sems,
    pack_send,
    pack_recv,
    start_send,
    start_recv,
    part_send,
    part_recv,
):
    row = lax.axis_index("row")
    col = lax.axis_index("col")
    rep = lax.axis_index("rep")
    plane = rows * cols
    place = row * cols + col
    slots, side, _ = raw_ref.shape

    def plane_peer(step):
        other = lax.rem(place + step, plane)
        return other, {"row": other // cols, "col": lax.rem(other, cols)}

    def rep_peer(step):
        other = lax.rem(rep + step, reps)
        return other, {"rep": other}

    barrier = pltpu.get_barrier_semaphore()
    for step in range(1, reps):
        pl.semaphore_signal(barrier, inc=1, device_id=rep_peer(step)[1], device_id_type=MESH)
    for step in range(1, plane):
        pl.semaphore_signal(barrier, inc=1, device_id=plane_peer(step)[1], device_id_type=MESH)

    loads = [
        pltpu.make_async_copy(codes_hbm, codes_ref, local_sems.at[0]),
        pltpu.make_async_copy(tiles_hbm, raw_ref, local_sems.at[1]),
        pltpu.make_async_copy(vectors_hbm, start_ref.at[place], local_sems.at[2]),
        pltpu.make_async_copy(energies_hbm, energies_ref, local_sems.at[3]),
    ]
    for load in loads:
        load.start()
    loads[0].wait()
    loads[1].wait()
    line = lax.broadcasted_iota(jnp.int32, (side, side), 0)
    lane = lax.broadcasted_iota(jnp.int32, (side, side), 1)
    diagonal_code = col * rows + row
    for slot in range(slots):
        code = jnp.full((side, side), codes_ref[slot], jnp.int32)
        keep = (code >= 0) & ((lane > line) | (code != diagonal_code))
        tile = jnp.where(keep, raw_ref[slot].astype(jnp.float32), 0.0)
        pack_ref[rep, slot, :side] = tile.astype(jnp.bfloat16)
        pack_ref[rep, slot, side:] = code[:CODE_ROWS].astype(jnp.float32).astype(jnp.bfloat16)
    loads[2].wait()
    loads[3].wait()
    pl.semaphore_wait(barrier, reps - 1 + plane - 1)

    sends = []
    for step in range(1, reps):
        other, device = rep_peer(step)
        copy = pltpu.make_async_remote_copy(
            src_ref=pack_ref.at[rep],
            dst_ref=pack_ref.at[rep],
            send_sem=pack_send.at[step],
            recv_sem=pack_recv.at[rep],
            device_id=device,
            device_id_type=MESH,
        )
        copy.start()
        sends.append(copy)

    def spread(buffer, send_sems, recv_sems):
        for step in range(1, plane):
            other, device = plane_peer(step)
            copy = pltpu.make_async_remote_copy(
                src_ref=buffer.at[place],
                dst_ref=buffer.at[place],
                send_sem=send_sems.at[step],
                recv_sem=recv_sems.at[place],
                device_id=device,
                device_id_type=MESH,
            )
            copy.start()
            sends.append(copy)

    def collect(buffer, recv_sems):
        for step in range(1, plane):
            other, device = plane_peer(step)
            pltpu.make_async_remote_copy(
                src_ref=buffer.at[other],
                dst_ref=buffer.at[other],
                send_sem=recv_sems.at[other],
                recv_sem=recv_sems.at[other],
                device_id=device,
                device_id_type=MESH,
            ).wait_recv()

    spread(start_ref, start_send, start_recv)

    def place_tiles(source, first):
        for slot in range(slots):
            tile = pack_ref[source, slot, :side].reshape(side // CODE_ROWS, CODE_ROWS, side)
            code = pack_ref[source, slot, side:].astype(jnp.float32)
            for a in range(cols):
                for k in range(rows):
                    spot = jnp.where(code == float(a * rows + k), 1.0, 0.0).astype(jnp.bfloat16)
                    term = (tile * spot[None]).reshape(side, side)
                    here = (pl.ds(a * side, side), pl.ds(k * side, side))
                    if first and slot == 0:
                        dense_ref[here] = term
                    else:
                        dense_ref[here] = dense_ref[here] + term

    place_tiles(rep, True)
    collect(start_ref, start_recv)
    for step in range(1, reps):
        other, device = rep_peer(step)
        pltpu.make_async_remote_copy(
            src_ref=pack_ref.at[other],
            dst_ref=pack_ref.at[other],
            send_sem=pack_recv.at[other],
            recv_sem=pack_recv.at[other],
            device_id=device,
            device_id_type=MESH,
        ).wait_recv()
        place_tiles(other, False)

    energies = energies_ref[...]

    def product(phase, state, scale, own_term):
        column_part = jnp.concatenate([state[k * cols + col] for k in range(rows)], axis=1)
        row_part = jnp.concatenate([state[row * cols + a] for a in range(cols)], axis=1)
        direct = lax.dot_general(
            column_part.astype(jnp.bfloat16),
            dense_ref[...],
            (((1,), (1,)), ((), ())),
            preferred_element_type=jnp.float32,
        )
        mirror = lax.dot_general(
            row_part.astype(jnp.bfloat16),
            dense_ref[...],
            (((1,), (0,)), ((), ())),
            preferred_element_type=jnp.float32,
        )
        buffer = part_ref.at[phase]
        for a in range(cols):
            owned = jnp.where(col == a, own_term, 0.0)
            buffer[place, a] = direct[:, a * side : (a + 1) * side] * scale + owned
        for k in range(rows):
            buffer[place, cols + k] = mirror[:, k * side : (k + 1) * side] * scale
        spread(buffer, part_send.at[phase], part_recv.at[phase])
        collect(buffer, part_recv.at[phase])
        totals = []
        for block in range(plane):
            terms = []
            for c in range(cols):
                terms.append(buffer[(block // cols) * cols + c, block % cols])
            for r in range(rows):
                terms.append(buffer[r * cols + block % cols, cols + block // cols])
            total = terms[0]
            for term in terms[1:]:
                total = total + term
            totals.append(total)
        return totals

    scale = sigma_first / half
    start_own = start_ref[place]
    latest = product(0, start_ref, scale, (energies * start_own - centre * start_own) * scale)
    for block in range(plane):
        state_ref[0, block] = latest[block]
    scale = 2.0 * sigma_next / half
    own = state_ref[0, place]
    newest = product(
        1,
        state_ref.at[0],
        scale,
        (energies * own - centre * own) * scale - sigma_first * sigma_next * start_own,
    )
    for block in range(plane):
        state_ref[1, block] = newest[block]
    own = state_ref[1, place]
    image = product(2, state_ref.at[1], 1.0, energies * own)
    for block in range(plane):
        state_ref[2, block] = image[block]
    squares = newest[0] * newest[0]
    crossed = newest[0] * image[0]
    for block in range(1, plane):
        squares = squares + newest[block] * newest[block]
        crossed = crossed + newest[block] * image[block]
    ritz = jnp.sum(crossed, axis=1, keepdims=True) / (
        jnp.sum(squares, axis=1, keepdims=True) + 1e-06
    )
    resid = state_ref[2, place] - ritz * own
    spacing = energies - ritz
    result_ref[0] = own - spacing / jnp.maximum(spacing * spacing, 1.0) * resid
    result_ref[1] = jnp.broadcast_to(ritz, own.shape)
    for copy in sends:
        copy.wait_send()


def fused(vectors, energies, tiles, tile_codes):
    rows = lax.axis_size("row")
    cols = lax.axis_size("col")
    reps = lax.axis_size("rep")
    plane = rows * cols
    local_count = vectors.shape[0]
    slots, side, _ = tiles.shape
    vector_shape = (local_count, side)
    result = pl.pallas_call(
        functools.partial(fused_kernel, rows, cols, reps),
        out_shape=pltpu.VMEM((2,) + vector_shape, jnp.float32),
        in_specs=[pl.BlockSpec(memory_space=pl.ANY)] * 4,
        out_specs=pl.BlockSpec(memory_space=pltpu.VMEM),
        scratch_shapes=[
            pltpu.VMEM((1, side), jnp.float32),
            pltpu.VMEM((slots, side, side), jnp.bfloat16),
            pltpu.SMEM((slots,), jnp.int32),
            pltpu.VMEM((reps, slots, side + CODE_ROWS, side), jnp.bfloat16),
            pltpu.VMEM((plane,) + vector_shape, jnp.float32),
            pltpu.VMEM((cols * side, rows * side), jnp.bfloat16),
            pltpu.VMEM((3, plane) + vector_shape, jnp.float32),
            pltpu.VMEM((3, plane, cols + rows) + vector_shape, jnp.float32),
            pltpu.SemaphoreType.DMA((4,)),
            pltpu.SemaphoreType.DMA((reps,)),
            pltpu.SemaphoreType.DMA((reps,)),
            pltpu.SemaphoreType.DMA((plane,)),
            pltpu.SemaphoreType.DMA((plane,)),
            pltpu.SemaphoreType.DMA((3, plane)),
            pltpu.SemaphoreType.DMA((3, plane)),
        ],
        compiler_params=pltpu.CompilerParams(collective_id=0, has_side_effects=True),
    )(vectors, energies.reshape(1, side), tiles, tile_codes)
    return result[0], result[1, :, 0]


def collective_form(vectors, energies, tiles, tile_codes):
    rows_count = lax.axis_size("row")
    cols_count = lax.axis_size("col")
    reps_count = lax.axis_size("rep")
    row_index = lax.axis_index("row")
    col_index = lax.axis_index("col")
    tile_side = tiles.shape[1]
    local_count = vectors.shape[0]
    total_count = local_count * reps_count
    present = tile_codes >= 0
    safe_code = jnp.where(present, tile_codes, 0)
    block_row = safe_code // rows_count
    block_col = safe_code % rows_count
    on_diagonal = present & (block_row == col_index) & (block_col == row_index)
    upper_mask = lax.broadcasted_iota(jnp.int32, (tile_side, tile_side), 1) > lax.broadcasted_iota(
        jnp.int32, (tile_side, tile_side), 0
    )
    keep_mask = present[:, None, None] & (
        upper_mask[None] | jnp.logical_not(on_diagonal)[:, None, None]
    )
    stored = jnp.where(keep_mask, tiles, jnp.zeros((), tiles.dtype))
    row_select = jnp.where(
        present[:, None] & (block_row[:, None] == jnp.arange(cols_count)[None, :]), 1.0, 0.0
    ).astype(jnp.float32)
    col_select = jnp.where(
        present[:, None] & (block_col[:, None] == jnp.arange(rows_count)[None, :]), 1.0, 0.0
    ).astype(jnp.float32)

    def chosen(select, group):
        picked = jnp.einsum(
            "sk,kvj->svj",
            select.astype(group.dtype),
            group,
            preferred_element_type=jnp.float32,
        )
        return picked.astype(group.dtype)

    def product(vector_block):
        rounded = vector_block.astype(jnp.bfloat16)[None]
        row_group = lax.all_gather(rounded, ("col", "rep"), axis=0, tiled=True).reshape(
            cols_count, total_count, tile_side
        )
        col_group = lax.all_gather(rounded, ("row", "rep"), axis=0, tiled=True).reshape(
            rows_count, total_count, tile_side
        )
        direct = jnp.einsum(
            "svj,sij->svi", chosen(col_select, col_group), stored, preferred_element_type=jnp.float32
        )
        mirror = jnp.einsum(
            "svi,sij->svj", chosen(row_select, row_group), stored, preferred_element_type=jnp.float32
        )
        row_terms = jnp.einsum("sa,svi->avi", row_select, direct, precision=lax.Precision.HIGHEST)
        col_terms = jnp.einsum("sk,svj->kvj", col_select, mirror, precision=lax.Precision.HIGHEST)
        row_total = lax.psum_scatter(
            row_terms.reshape(cols_count * reps_count, local_count, tile_side),
            ("col", "rep"),
            scatter_dimension=0,
            tiled=True,
        )[0]
        partial_rows = lax.psum_scatter(col_terms, "row", scatter_dimension=0, tiled=True)
        col_total = lax.psum_scatter(partial_rows, "rep", scatter_dimension=1, tiled=True)[0]
        return energies[None, :] * vector_block + row_total + col_total

    half = (filter_top - filter_low) / 2.0
    centre = (filter_top + filter_low) / 2.0
    sigma_first = half / (spectrum_low - centre)
    tau_value = 2.0 / sigma_first
    current = vectors
    previous = current
    latest = (product(current) - centre * current) * (sigma_first / half)
    sigma_next = 1.0 / (tau_value - sigma_first)
    newest = (product(latest) - centre * latest) * (
        2.0 * sigma_next / half
    ) - sigma_first * sigma_next * previous
    current = newest
    image = product(current)
    squares, crossed = lax.psum(
        (jnp.sum(current * current, axis=1), jnp.sum(current * image, axis=1)), ("row", "col")
    )
    ritz = crossed / (squares + 1e-06)
    resid = image - ritz[:, None] * current
    spacing = energies[None, :] - ritz[:, None]
    current = current - spacing / jnp.maximum(spacing * spacing, 1.0) * resid
    return (current, ritz)


def on_device(vectors, energies, tiles, tile_codes):
    plane = lax.axis_size("row") * lax.axis_size("col")
    placed = lax.axis_size("rep") * tiles.shape[0] * plane
    if placed <= 256 and energies.shape[0] == tiles.shape[1]:
        return fused(vectors, energies, tiles, tile_codes)
    return collective_form(vectors, energies, tiles, tile_codes)


def solution(mesh):
    in_specs = (
        P("rep", ("row", "col")),
        P(("row", "col")),
        P(("row", "col", "rep"), None, None),
        P(("row", "col", "rep")),
    )
    out_specs = (P("rep", ("row", "col")), P("rep"))
    return jax.shard_map(
        on_device, mesh=mesh, in_specs=in_specs, out_specs=out_specs, check_vma=False
    )
```

```python
import functools

import jax
import jax.numpy as jnp
from jax import lax
from jax.experimental import pallas as pl
from jax.experimental.pallas import tpu as pltpu
from jax.sharding import PartitionSpec as P

filter_low = 5.0
filter_top = 20.0
spectrum_low = -3.0

half = (filter_top - filter_low) / 2.0
centre = (filter_top + filter_low) / 2.0
sigma_first = half / (spectrum_low - centre)
tau_value = 2.0 / sigma_first
sigma_next = 1.0 / (tau_value - sigma_first)

MESH = pl.DeviceIdType.MESH
CODE_ROWS = 16


def fused_kernel(
    rows,
    cols,
    reps,
    vectors_hbm,
    energies_hbm,
    tiles_hbm,
    codes_hbm,
    result_ref,
    energies_ref,
    raw_ref,
    codes_ref,
    pack_ref,
    start_ref,
    dense_ref,
    state_ref,
    part_ref,
    local_sems,
    pack_send,
    pack_recv,
    start_send,
    start_recv,
    part_send,
    part_recv,
):
    row = lax.axis_index("row")
    col = lax.axis_index("col")
    rep = lax.axis_index("rep")
    plane = rows * cols
    place = row * cols + col
    slots, side, _ = raw_ref.shape

    def plane_peer(step):
        other = lax.rem(place + step, plane)
        return other, {"row": other // cols, "col": lax.rem(other, cols)}

    def rep_peer(step):
        other = lax.rem(rep + step, reps)
        return other, {"rep": other}

    barrier = pltpu.get_barrier_semaphore()
    for step in range(1, reps):
        pl.semaphore_signal(barrier, inc=1, device_id=rep_peer(step)[1], device_id_type=MESH)
    for step in range(1, plane):
        pl.semaphore_signal(barrier, inc=1, device_id=plane_peer(step)[1], device_id_type=MESH)

    loads = [
        pltpu.make_async_copy(codes_hbm, codes_ref, local_sems.at[0]),
        pltpu.make_async_copy(tiles_hbm, raw_ref, local_sems.at[1]),
        pltpu.make_async_copy(vectors_hbm, start_ref.at[place], local_sems.at[2]),
        pltpu.make_async_copy(energies_hbm, energies_ref, local_sems.at[3]),
    ]
    for load in loads:
        load.start()
    loads[0].wait()
    loads[1].wait()
    line = lax.broadcasted_iota(jnp.int32, (side, side), 0)
    lane = lax.broadcasted_iota(jnp.int32, (side, side), 1)
    diagonal_code = col * rows + row
    for slot in range(slots):
        code = jnp.full((side, side), codes_ref[slot], jnp.int32)
        keep = (code >= 0) & ((lane > line) | (code != diagonal_code))
        tile = jnp.where(keep, raw_ref[slot].astype(jnp.float32), 0.0)
        pack_ref[rep, slot, :side] = tile.astype(jnp.bfloat16)
        pack_ref[rep, slot, side:] = code[:CODE_ROWS].astype(jnp.float32).astype(jnp.bfloat16)
    loads[2].wait()
    loads[3].wait()
    pl.semaphore_wait(barrier, reps - 1 + plane - 1)

    sends = []
    for step in range(1, reps):
        other, device = rep_peer(step)
        copy = pltpu.make_async_remote_copy(
            src_ref=pack_ref.at[rep],
            dst_ref=pack_ref.at[rep],
            send_sem=pack_send.at[step],
            recv_sem=pack_recv.at[rep],
            device_id=device,
            device_id_type=MESH,
        )
        copy.start()
        sends.append(copy)

    def spread(buffer, send_sems, recv_sems):
        for step in range(1, plane):
            other, device = plane_peer(step)
            copy = pltpu.make_async_remote_copy(
                src_ref=buffer.at[place],
                dst_ref=buffer.at[place],
                send_sem=send_sems.at[step],
                recv_sem=recv_sems.at[place],
                device_id=device,
                device_id_type=MESH,
            )
            copy.start()
            sends.append(copy)

    def collect(buffer, recv_sems):
        for step in range(1, plane):
            other, device = plane_peer(step)
            pltpu.make_async_remote_copy(
                src_ref=buffer.at[other],
                dst_ref=buffer.at[other],
                send_sem=recv_sems.at[other],
                recv_sem=recv_sems.at[other],
                device_id=device,
                device_id_type=MESH,
            ).wait_recv()

    spread(start_ref, start_send, start_recv)

    def place_tiles(source, first):
        for slot in range(slots):
            tile = pack_ref[source, slot, :side].reshape(side // CODE_ROWS, CODE_ROWS, side)
            code = pack_ref[source, slot, side:].astype(jnp.float32)
            for a in range(cols):
                for k in range(rows):
                    spot = jnp.where(code == float(a * rows + k), 1.0, 0.0).astype(jnp.bfloat16)
                    term = (tile * spot[None]).reshape(side, side)
                    here = (pl.ds(a * side, side), pl.ds(k * side, side))
                    if first and slot == 0:
                        dense_ref[here] = term
                    else:
                        dense_ref[here] = dense_ref[here] + term

    place_tiles(rep, True)
    collect(start_ref, start_recv)
    for step in range(1, reps):
        other, device = rep_peer(step)
        pltpu.make_async_remote_copy(
            src_ref=pack_ref.at[other],
            dst_ref=pack_ref.at[other],
            send_sem=pack_recv.at[other],
            recv_sem=pack_recv.at[other],
            device_id=device,
            device_id_type=MESH,
        ).wait_recv()
        place_tiles(other, False)

    energies = energies_ref[...]

    def product(phase, state, scale, own_term):
        column_part = jnp.concatenate([state[k * cols + col] for k in range(rows)], axis=1)
        row_part = jnp.concatenate([state[row * cols + a] for a in range(cols)], axis=1)
        direct = lax.dot_general(
            column_part.astype(jnp.bfloat16),
            dense_ref[...],
            (((1,), (1,)), ((), ())),
            preferred_element_type=jnp.float32,
        )
        mirror = lax.dot_general(
            row_part.astype(jnp.bfloat16),
            dense_ref[...],
            (((1,), (0,)), ((), ())),
            preferred_element_type=jnp.float32,
        )
        buffer = part_ref.at[phase]
        for a in range(cols):
            owned = jnp.where(col == a, own_term, 0.0)
            buffer[place, a] = direct[:, a * side : (a + 1) * side] * scale + owned
        for k in range(rows):
            buffer[place, cols + k] = mirror[:, k * side : (k + 1) * side] * scale
        spread(buffer, part_send.at[phase], part_recv.at[phase])
        collect(buffer, part_recv.at[phase])
        totals = []
        for block in range(plane):
            terms = []
            for c in range(cols):
                terms.append(buffer[(block // cols) * cols + c, block % cols])
            for r in range(rows):
                terms.append(buffer[r * cols + block % cols, cols + block // cols])
            total = terms[0]
            for term in terms[1:]:
                total = total + term
            totals.append(total)
        return totals

    scale = sigma_first / half
    start_own = start_ref[place]
    latest = product(0, start_ref, scale, (energies * start_own - centre * start_own) * scale)
    for block in range(plane):
        state_ref[0, block] = latest[block]
    scale = 2.0 * sigma_next / half
    own = state_ref[0, place]
    newest = product(
        1,
        state_ref.at[0],
        scale,
        (energies * own - centre * own) * scale - sigma_first * sigma_next * start_own,
    )
    for block in range(plane):
        state_ref[1, block] = newest[block]
    own = state_ref[1, place]
    image = product(2, state_ref.at[1], 1.0, energies * own)
    for block in range(plane):
        state_ref[2, block] = image[block]
    squares = newest[0] * newest[0]
    crossed = newest[0] * image[0]
    for block in range(1, plane):
        squares = squares + newest[block] * newest[block]
        crossed = crossed + newest[block] * image[block]
    ritz = jnp.sum(crossed, axis=1, keepdims=True) / (
        jnp.sum(squares, axis=1, keepdims=True) + 1e-06
    )
    resid = state_ref[2, place] - ritz * own
    spacing = energies - ritz
    result_ref[0] = own - spacing / jnp.maximum(spacing * spacing, 1.0) * resid
    result_ref[1] = jnp.broadcast_to(ritz, own.shape)
    for copy in sends:
        copy.wait_send()


def output_kernel(result_ref, filtered_ref, ritz_ref):
    filtered_ref[...] = result_ref[0]
    for vector in range(ritz_ref.shape[0]):
        ritz_ref[vector] = result_ref[1, vector, 0]


def fused(vectors, energies, tiles, tile_codes):
    rows = lax.axis_size("row")
    cols = lax.axis_size("col")
    reps = lax.axis_size("rep")
    plane = rows * cols
    local_count = vectors.shape[0]
    slots, side, _ = tiles.shape
    vector_shape = (local_count, side)
    result = pl.pallas_call(
        functools.partial(fused_kernel, rows, cols, reps),
        out_shape=pltpu.VMEM((2,) + vector_shape, jnp.float32),
        in_specs=[pl.BlockSpec(memory_space=pl.ANY)] * 4,
        out_specs=pl.BlockSpec(memory_space=pltpu.VMEM),
        scratch_shapes=[
            pltpu.VMEM((1, side), jnp.float32),
            pltpu.VMEM((slots, side, side), jnp.bfloat16),
            pltpu.SMEM((slots,), jnp.int32),
            pltpu.VMEM((reps, slots, side + CODE_ROWS, side), jnp.bfloat16),
            pltpu.VMEM((plane,) + vector_shape, jnp.float32),
            pltpu.VMEM((cols * side, rows * side), jnp.bfloat16),
            pltpu.VMEM((3, plane) + vector_shape, jnp.float32),
            pltpu.VMEM((3, plane, cols + rows) + vector_shape, jnp.float32),
            pltpu.SemaphoreType.DMA((4,)),
            pltpu.SemaphoreType.DMA((reps,)),
            pltpu.SemaphoreType.DMA((reps,)),
            pltpu.SemaphoreType.DMA((plane,)),
            pltpu.SemaphoreType.DMA((plane,)),
            pltpu.SemaphoreType.DMA((3, plane)),
            pltpu.SemaphoreType.DMA((3, plane)),
        ],
        compiler_params=pltpu.CompilerParams(collective_id=0, has_side_effects=True),
    )(vectors, energies.reshape(1, side), tiles, tile_codes)
    return pl.pallas_call(
        output_kernel,
        out_shape=(
            jax.ShapeDtypeStruct(vector_shape, jnp.float32),
            jax.ShapeDtypeStruct((local_count,), jnp.float32),
        ),
        in_specs=[pl.BlockSpec(memory_space=pltpu.VMEM)],
        out_specs=(
            pl.BlockSpec(memory_space=pltpu.VMEM),
            pl.BlockSpec(memory_space=pltpu.SMEM),
        ),
    )(pltpu.with_memory_space_constraint(result, pltpu.VMEM))


def collective_form(vectors, energies, tiles, tile_codes):
    rows_count = lax.axis_size("row")
    cols_count = lax.axis_size("col")
    reps_count = lax.axis_size("rep")
    row_index = lax.axis_index("row")
    col_index = lax.axis_index("col")
    tile_side = tiles.shape[1]
    local_count = vectors.shape[0]
    total_count = local_count * reps_count
    present = tile_codes >= 0
    safe_code = jnp.where(present, tile_codes, 0)
    block_row = safe_code // rows_count
    block_col = safe_code % rows_count
    on_diagonal = present & (block_row == col_index) & (block_col == row_index)
    upper_mask = lax.broadcasted_iota(jnp.int32, (tile_side, tile_side), 1) > lax.broadcasted_iota(
        jnp.int32, (tile_side, tile_side), 0
    )
    keep_mask = present[:, None, None] & (
        upper_mask[None] | jnp.logical_not(on_diagonal)[:, None, None]
    )
    stored = jnp.where(keep_mask, tiles, jnp.zeros((), tiles.dtype))
    row_select = jnp.where(
        present[:, None] & (block_row[:, None] == jnp.arange(cols_count)[None, :]), 1.0, 0.0
    ).astype(jnp.float32)
    col_select = jnp.where(
        present[:, None] & (block_col[:, None] == jnp.arange(rows_count)[None, :]), 1.0, 0.0
    ).astype(jnp.float32)

    def chosen(select, group):
        picked = jnp.einsum(
            "sk,kvj->svj",
            select.astype(group.dtype),
            group,
            preferred_element_type=jnp.float32,
        )
        return picked.astype(group.dtype)

    def product(vector_block):
        rounded = vector_block.astype(jnp.bfloat16)[None]
        row_group = lax.all_gather(rounded, ("col", "rep"), axis=0, tiled=True).reshape(
            cols_count, total_count, tile_side
        )
        col_group = lax.all_gather(rounded, ("row", "rep"), axis=0, tiled=True).reshape(
            rows_count, total_count, tile_side
        )
        direct = jnp.einsum(
            "svj,sij->svi", chosen(col_select, col_group), stored, preferred_element_type=jnp.float32
        )
        mirror = jnp.einsum(
            "svi,sij->svj", chosen(row_select, row_group), stored, preferred_element_type=jnp.float32
        )
        row_terms = jnp.einsum("sa,svi->avi", row_select, direct, precision=lax.Precision.HIGHEST)
        col_terms = jnp.einsum("sk,svj->kvj", col_select, mirror, precision=lax.Precision.HIGHEST)
        row_total = lax.psum_scatter(
            row_terms.reshape(cols_count * reps_count, local_count, tile_side),
            ("col", "rep"),
            scatter_dimension=0,
            tiled=True,
        )[0]
        partial_rows = lax.psum_scatter(col_terms, "row", scatter_dimension=0, tiled=True)
        col_total = lax.psum_scatter(partial_rows, "rep", scatter_dimension=1, tiled=True)[0]
        return energies[None, :] * vector_block + row_total + col_total

    half = (filter_top - filter_low) / 2.0
    centre = (filter_top + filter_low) / 2.0
    sigma_first = half / (spectrum_low - centre)
    tau_value = 2.0 / sigma_first
    current = vectors
    previous = current
    latest = (product(current) - centre * current) * (sigma_first / half)
    sigma_next = 1.0 / (tau_value - sigma_first)
    newest = (product(latest) - centre * latest) * (
        2.0 * sigma_next / half
    ) - sigma_first * sigma_next * previous
    current = newest
    image = product(current)
    squares, crossed = lax.psum(
        (jnp.sum(current * current, axis=1), jnp.sum(current * image, axis=1)), ("row", "col")
    )
    ritz = crossed / (squares + 1e-06)
    resid = image - ritz[:, None] * current
    spacing = energies[None, :] - ritz[:, None]
    current = current - spacing / jnp.maximum(spacing * spacing, 1.0) * resid
    return (current, ritz)


def on_device(vectors, energies, tiles, tile_codes):
    plane = lax.axis_size("row") * lax.axis_size("col")
    placed = lax.axis_size("rep") * tiles.shape[0] * plane
    if placed <= 256 and energies.shape[0] == tiles.shape[1]:
        return fused(vectors, energies, tiles, tile_codes)
    return collective_form(vectors, energies, tiles, tile_codes)


def solution(mesh):
    in_specs = (
        P("rep", ("row", "col")),
        P(("row", "col")),
        P(("row", "col", "rep"), None, None),
        P(("row", "col", "rep")),
    )
    out_specs = (P("rep", ("row", "col")), P("rep"))
    return jax.shard_map(
        on_device, mesh=mesh, in_specs=in_specs, out_specs=out_specs, check_vma=False
    )
```

```python
import functools

import jax
import jax.numpy as jnp
from jax import lax
from jax.experimental import pallas as pl
from jax.experimental.pallas import tpu as pltpu
from jax.sharding import PartitionSpec as P

filter_low = 5.0
filter_top = 20.0
spectrum_low = -3.0

half = (filter_top - filter_low) / 2.0
centre = (filter_top + filter_low) / 2.0
sigma_first = half / (spectrum_low - centre)
tau_value = 2.0 / sigma_first
sigma_next = 1.0 / (tau_value - sigma_first)

MESH = pl.DeviceIdType.MESH
CODE_ROWS = 16


def fused_kernel(
    rows,
    cols,
    reps,
    vectors_hbm,
    energies_hbm,
    tiles_hbm,
    codes_hbm,
    result_ref,
    energies_ref,
    raw_ref,
    codes_ref,
    pack_ref,
    start_ref,
    dense_ref,
    state_ref,
    part_ref,
    local_sems,
    pack_send,
    pack_recv,
    start_send,
    start_recv,
    part_send,
    part_recv,
):
    row = lax.axis_index("row")
    col = lax.axis_index("col")
    rep = lax.axis_index("rep")
    plane = rows * cols
    place = row * cols + col
    slots, side, _ = raw_ref.shape

    def plane_peer(step):
        other = lax.rem(place + step, plane)
        return other, {"row": other // cols, "col": lax.rem(other, cols)}

    def rep_peer(step):
        other = lax.rem(rep + step, reps)
        return other, {"rep": other}

    barrier = pltpu.get_barrier_semaphore()
    for step in range(1, reps):
        pl.semaphore_signal(barrier, inc=1, device_id=rep_peer(step)[1], device_id_type=MESH)
    for step in range(1, plane):
        pl.semaphore_signal(barrier, inc=1, device_id=plane_peer(step)[1], device_id_type=MESH)

    loads = [
        pltpu.make_async_copy(codes_hbm, codes_ref, local_sems.at[0]),
        pltpu.make_async_copy(tiles_hbm, raw_ref, local_sems.at[1]),
        pltpu.make_async_copy(vectors_hbm, start_ref.at[place], local_sems.at[2]),
        pltpu.make_async_copy(energies_hbm, energies_ref, local_sems.at[3]),
    ]
    for load in loads:
        load.start()
    loads[0].wait()
    loads[1].wait()
    line = lax.broadcasted_iota(jnp.int32, (side, side), 0)
    lane = lax.broadcasted_iota(jnp.int32, (side, side), 1)
    diagonal_code = col * rows + row
    for slot in range(slots):
        code = jnp.full((side, side), codes_ref[slot], jnp.int32)
        keep = (code >= 0) & ((lane > line) | (code != diagonal_code))
        tile = jnp.where(keep, raw_ref[slot].astype(jnp.float32), 0.0)
        pack_ref[rep, slot, :side] = tile.astype(jnp.bfloat16)
        pack_ref[rep, slot, side:] = code[:CODE_ROWS].astype(jnp.float32).astype(jnp.bfloat16)
    pl.semaphore_wait(barrier, reps - 1 + plane - 1)

    sends = []
    for step in range(1, reps):
        other, device = rep_peer(step)
        copy = pltpu.make_async_remote_copy(
            src_ref=pack_ref.at[rep],
            dst_ref=pack_ref.at[rep],
            send_sem=pack_send.at[step],
            recv_sem=pack_recv.at[rep],
            device_id=device,
            device_id_type=MESH,
        )
        copy.start()
        sends.append(copy)

    def spread(buffer, send_sems, recv_sems):
        for step in range(1, plane):
            other, device = plane_peer(step)
            copy = pltpu.make_async_remote_copy(
                src_ref=buffer.at[place],
                dst_ref=buffer.at[place],
                send_sem=send_sems.at[step],
                recv_sem=recv_sems.at[place],
                device_id=device,
                device_id_type=MESH,
            )
            copy.start()
            sends.append(copy)

    def collect(buffer, recv_sems):
        for step in range(1, plane):
            other, device = plane_peer(step)
            pltpu.make_async_remote_copy(
                src_ref=buffer.at[other],
                dst_ref=buffer.at[other],
                send_sem=recv_sems.at[other],
                recv_sem=recv_sems.at[other],
                device_id=device,
                device_id_type=MESH,
            ).wait_recv()

    loads[2].wait()
    spread(start_ref, start_send, start_recv)

    def place_tiles(source, first):
        for slot in range(slots):
            tile = pack_ref[source, slot, :side].reshape(side // CODE_ROWS, CODE_ROWS, side)
            code = pack_ref[source, slot, side:].astype(jnp.float32)
            for a in range(cols):
                for k in range(rows):
                    spot = jnp.where(code == float(a * rows + k), 1.0, 0.0).astype(jnp.bfloat16)
                    term = (tile * spot[None]).reshape(side, side)
                    here = (pl.ds(a * side, side), pl.ds(k * side, side))
                    if first and slot == 0:
                        dense_ref[here] = term
                    else:
                        dense_ref[here] = dense_ref[here] + term

    place_tiles(rep, True)
    collect(start_ref, start_recv)
    for step in range(1, reps):
        other, device = rep_peer(step)
        pltpu.make_async_remote_copy(
            src_ref=pack_ref.at[other],
            dst_ref=pack_ref.at[other],
            send_sem=pack_recv.at[other],
            recv_sem=pack_recv.at[other],
            device_id=device,
            device_id_type=MESH,
        ).wait_recv()
        place_tiles(other, False)

    loads[3].wait()
    energies = energies_ref[...]

    def product(phase, state, scale, own_term):
        column_part = jnp.concatenate([state[k * cols + col] for k in range(rows)], axis=1)
        row_part = jnp.concatenate([state[row * cols + a] for a in range(cols)], axis=1)
        direct = lax.dot_general(
            column_part.astype(jnp.bfloat16),
            dense_ref[...],
            (((1,), (1,)), ((), ())),
            preferred_element_type=jnp.float32,
        )
        mirror = lax.dot_general(
            row_part.astype(jnp.bfloat16),
            dense_ref[...],
            (((1,), (0,)), ((), ())),
            preferred_element_type=jnp.float32,
        )
        buffer = part_ref.at[phase]
        for a in range(cols):
            owned = jnp.where(col == a, own_term, 0.0)
            buffer[place, a] = direct[:, a * side : (a + 1) * side] * scale + owned
        for k in range(rows):
            buffer[place, cols + k] = mirror[:, k * side : (k + 1) * side] * scale
        spread(buffer, part_send.at[phase], part_recv.at[phase])
        collect(buffer, part_recv.at[phase])
        totals = []
        for block in range(plane):
            terms = []
            for c in range(cols):
                terms.append(buffer[(block // cols) * cols + c, block % cols])
            for r in range(rows):
                terms.append(buffer[r * cols + block % cols, cols + block // cols])
            total = terms[0]
            for term in terms[1:]:
                total = total + term
            totals.append(total)
        return totals

    scale = sigma_first / half
    start_own = start_ref[place]
    latest = product(0, start_ref, scale, (energies * start_own - centre * start_own) * scale)
    for block in range(plane):
        state_ref[0, block] = latest[block]
    scale = 2.0 * sigma_next / half
    own = state_ref[0, place]
    newest = product(
        1,
        state_ref.at[0],
        scale,
        (energies * own - centre * own) * scale - sigma_first * sigma_next * start_own,
    )
    for block in range(plane):
        state_ref[1, block] = newest[block]
    own = state_ref[1, place]
    image = product(2, state_ref.at[1], 1.0, energies * own)
    for block in range(plane):
        state_ref[2, block] = image[block]
    squares = newest[0] * newest[0]
    crossed = newest[0] * image[0]
    for block in range(1, plane):
        squares = squares + newest[block] * newest[block]
        crossed = crossed + newest[block] * image[block]
    ritz = jnp.sum(crossed, axis=1, keepdims=True) / (
        jnp.sum(squares, axis=1, keepdims=True) + 1e-06
    )
    resid = state_ref[2, place] - ritz * own
    spacing = energies - ritz
    result_ref[0] = own - spacing / jnp.maximum(spacing * spacing, 1.0) * resid
    result_ref[1] = jnp.broadcast_to(ritz, own.shape)
    for copy in sends:
        copy.wait_send()


def output_kernel(result_ref, filtered_ref, ritz_ref):
    filtered_ref[...] = result_ref[0]
    for vector in range(ritz_ref.shape[0]):
        ritz_ref[vector] = result_ref[1, vector, 0]


def fused(vectors, energies, tiles, tile_codes):
    rows = lax.axis_size("row")
    cols = lax.axis_size("col")
    reps = lax.axis_size("rep")
    plane = rows * cols
    local_count = vectors.shape[0]
    slots, side, _ = tiles.shape
    vector_shape = (local_count, side)
    result = pl.pallas_call(
        functools.partial(fused_kernel, rows, cols, reps),
        out_shape=pltpu.VMEM((2,) + vector_shape, jnp.float32),
        in_specs=[pl.BlockSpec(memory_space=pl.ANY)] * 4,
        out_specs=pl.BlockSpec(memory_space=pltpu.VMEM),
        scratch_shapes=[
            pltpu.VMEM((1, side), jnp.float32),
            pltpu.VMEM((slots, side, side), jnp.bfloat16),
            pltpu.SMEM((slots,), jnp.int32),
            pltpu.VMEM((reps, slots, side + CODE_ROWS, side), jnp.bfloat16),
            pltpu.VMEM((plane,) + vector_shape, jnp.float32),
            pltpu.VMEM((cols * side, rows * side), jnp.bfloat16),
            pltpu.VMEM((3, plane) + vector_shape, jnp.float32),
            pltpu.VMEM((3, plane, cols + rows) + vector_shape, jnp.float32),
            pltpu.SemaphoreType.DMA((4,)),
            pltpu.SemaphoreType.DMA((reps,)),
            pltpu.SemaphoreType.DMA((reps,)),
            pltpu.SemaphoreType.DMA((plane,)),
            pltpu.SemaphoreType.DMA((plane,)),
            pltpu.SemaphoreType.DMA((3, plane)),
            pltpu.SemaphoreType.DMA((3, plane)),
        ],
        compiler_params=pltpu.CompilerParams(collective_id=0, has_side_effects=True),
    )(vectors, energies.reshape(1, side), tiles, tile_codes)
    return pl.pallas_call(
        output_kernel,
        out_shape=(
            jax.ShapeDtypeStruct(vector_shape, jnp.float32),
            jax.ShapeDtypeStruct((local_count,), jnp.float32),
        ),
        in_specs=[pl.BlockSpec(memory_space=pltpu.VMEM)],
        out_specs=(
            pl.BlockSpec(memory_space=pltpu.VMEM),
            pl.BlockSpec(memory_space=pltpu.SMEM),
        ),
    )(pltpu.with_memory_space_constraint(result, pltpu.VMEM))


def collective_form(vectors, energies, tiles, tile_codes):
    rows_count = lax.axis_size("row")
    cols_count = lax.axis_size("col")
    reps_count = lax.axis_size("rep")
    row_index = lax.axis_index("row")
    col_index = lax.axis_index("col")
    tile_side = tiles.shape[1]
    local_count = vectors.shape[0]
    total_count = local_count * reps_count
    present = tile_codes >= 0
    safe_code = jnp.where(present, tile_codes, 0)
    block_row = safe_code // rows_count
    block_col = safe_code % rows_count
    on_diagonal = present & (block_row == col_index) & (block_col == row_index)
    upper_mask = lax.broadcasted_iota(jnp.int32, (tile_side, tile_side), 1) > lax.broadcasted_iota(
        jnp.int32, (tile_side, tile_side), 0
    )
    keep_mask = present[:, None, None] & (
        upper_mask[None] | jnp.logical_not(on_diagonal)[:, None, None]
    )
    stored = jnp.where(keep_mask, tiles, jnp.zeros((), tiles.dtype))
    row_select = jnp.where(
        present[:, None] & (block_row[:, None] == jnp.arange(cols_count)[None, :]), 1.0, 0.0
    ).astype(jnp.float32)
    col_select = jnp.where(
        present[:, None] & (block_col[:, None] == jnp.arange(rows_count)[None, :]), 1.0, 0.0
    ).astype(jnp.float32)

    def chosen(select, group):
        picked = jnp.einsum(
            "sk,kvj->svj",
            select.astype(group.dtype),
            group,
            preferred_element_type=jnp.float32,
        )
        return picked.astype(group.dtype)

    def product(vector_block):
        rounded = vector_block.astype(jnp.bfloat16)[None]
        row_group = lax.all_gather(rounded, ("col", "rep"), axis=0, tiled=True).reshape(
            cols_count, total_count, tile_side
        )
        col_group = lax.all_gather(rounded, ("row", "rep"), axis=0, tiled=True).reshape(
            rows_count, total_count, tile_side
        )
        direct = jnp.einsum(
            "svj,sij->svi", chosen(col_select, col_group), stored, preferred_element_type=jnp.float32
        )
        mirror = jnp.einsum(
            "svi,sij->svj", chosen(row_select, row_group), stored, preferred_element_type=jnp.float32
        )
        row_terms = jnp.einsum("sa,svi->avi", row_select, direct, precision=lax.Precision.HIGHEST)
        col_terms = jnp.einsum("sk,svj->kvj", col_select, mirror, precision=lax.Precision.HIGHEST)
        row_total = lax.psum_scatter(
            row_terms.reshape(cols_count * reps_count, local_count, tile_side),
            ("col", "rep"),
            scatter_dimension=0,
            tiled=True,
        )[0]
        partial_rows = lax.psum_scatter(col_terms, "row", scatter_dimension=0, tiled=True)
        col_total = lax.psum_scatter(partial_rows, "rep", scatter_dimension=1, tiled=True)[0]
        return energies[None, :] * vector_block + row_total + col_total

    half = (filter_top - filter_low) / 2.0
    centre = (filter_top + filter_low) / 2.0
    sigma_first = half / (spectrum_low - centre)
    tau_value = 2.0 / sigma_first
    current = vectors
    previous = current
    latest = (product(current) - centre * current) * (sigma_first / half)
    sigma_next = 1.0 / (tau_value - sigma_first)
    newest = (product(latest) - centre * latest) * (
        2.0 * sigma_next / half
    ) - sigma_first * sigma_next * previous
    current = newest
    image = product(current)
    squares, crossed = lax.psum(
        (jnp.sum(current * current, axis=1), jnp.sum(current * image, axis=1)), ("row", "col")
    )
    ritz = crossed / (squares + 1e-06)
    resid = image - ritz[:, None] * current
    spacing = energies[None, :] - ritz[:, None]
    current = current - spacing / jnp.maximum(spacing * spacing, 1.0) * resid
    return (current, ritz)


def on_device(vectors, energies, tiles, tile_codes):
    plane = lax.axis_size("row") * lax.axis_size("col")
    placed = lax.axis_size("rep") * tiles.shape[0] * plane
    if placed <= 256 and energies.shape[0] == tiles.shape[1]:
        return fused(vectors, energies, tiles, tile_codes)
    return collective_form(vectors, energies, tiles, tile_codes)


def solution(mesh):
    in_specs = (
        P("rep", ("row", "col")),
        P(("row", "col")),
        P(("row", "col", "rep"), None, None),
        P(("row", "col", "rep")),
    )
    out_specs = (P("rep", ("row", "col")), P("rep"))
    return jax.shard_map(
        on_device, mesh=mesh, in_specs=in_specs, out_specs=out_specs, check_vma=False
    )
```
